32 devices in a mesh: snp: 8 (over y, x, core), ind: 4 (over z).
Axes of the slice: x: 2, y: 2, z: 4, core: 2. Of those that a mesh axis runs over, the one named last changes fastest.
Arguments:
- genotypes: bfloat16 [8192, 4096], P('ind', 'snp'), may hold values from -12 to 12, as said below
- annotations: bfloat16 [4096, 512], P('snp'), may hold values from -0.3984375 to 0.3984375
- window_start: int32 [4096], P(('snp', 'ind')), may hold values from 0 to 4095, as said below
- window_end: int32 [4096], P(('snp', 'ind')), may hold values from 1 to 4096, as said below
Outputs:
- ld_scores: float32 [4096, 512], P(('snp', 'ind'))
The draws below stay inside these ranges and needn't reach their ends.
Inputs may be any that keep to these rules, and one draw needn't show every extreme that they name: `genotypes`: real-valued dosages, each SNP with its own scale; values within the range. For each SNP j: window_start(j) <= j; j - window_start(j) <= 512, reached on every draw; k is in the window of j exactly when j is in the window of k; never falls along the SNPs. For each SNP j: window_end(j) > j; window_end(j) - j <= 513, reached on every draw; never falls along the SNPs.
All inputs are finite; a program needn't handle non-finite values.
Results may differ from the reference program's by a relative error of at most 0.0033.
Values may be sent and summed in bfloat16 or wider, within the bound.
No kernel may reach another device: no remote copies, remote signals or barrier semaphores. Data moves between devices by JAX's collectives and lax.ppermute only.
A program may use at most 64 MiB of HBM per device.

```python
import jax
import jax.numpy as jnp
from jax import lax

S_DEV = 512
C = 512
SNPS = 4096
IND = 8192
N_SNP = 8


def draw_genotypes(key, part):
    subkeys = jax.random.split(key, 7)
    fine_len = S_DEV // 4
    fine_count = SNPS // fine_len + 2
    coarse_count = SNPS // S_DEV + 2
    shift_fine = jax.random.randint(subkeys[0], (), 0, fine_len)
    shift_coarse = jax.random.randint(subkeys[1], (), 0, S_DEV)
    indices = jnp.arange(SNPS, dtype=jnp.int32)
    fine_id = (indices + shift_fine) // fine_len
    coarse_id = (indices + shift_coarse) // S_DEV
    fine_latent = jax.random.normal(subkeys[2], (IND, fine_count), jnp.float32)
    coarse_latent = jax.random.normal(subkeys[3], (IND, coarse_count), jnp.float32)
    w_fine = jax.random.uniform(subkeys[4], (SNPS,), jnp.float32, 0.5, 1.5)
    w_coarse = jax.random.uniform(subkeys[5], (SNPS,), jnp.float32, 0.3, 1.0)
    noise_part = jax.random.normal(subkeys[6], (IND, SNPS), jnp.float32)
    values = fine_latent[:, fine_id] * w_fine + coarse_latent[:, coarse_id] * w_coarse + noise_part
    values = jnp.clip(values, -12.0, 12.0)
    return values.astype(jnp.bfloat16)


def window_bounds(key):
    first_key, second_key = jax.random.split(jax.random.fold_in(key, 11))
    increments = jax.random.randint(first_key, (SNPS,), 0, 4)
    cold_start = jax.random.randint(second_key, (), 0, SNPS - 2 * S_DEV - 1)
    indices = jnp.arange(SNPS, dtype=jnp.int32)
    increments = jnp.where((indices >= cold_start) & (indices <= cold_start + 2 * S_DEV), 0, increments)
    map_pos = jnp.cumsum(increments).astype(jnp.int32)
    map_unit = S_DEV // 2
    lower_edge = jnp.searchsorted(map_pos, map_pos - map_unit, side='left').astype(jnp.int32)
    upper_edge = jnp.searchsorted(map_pos, map_pos + map_unit, side='right').astype(jnp.int32)
    start_out = jnp.maximum(lower_edge, indices - S_DEV)
    end_out = jnp.minimum(upper_edge, indices + S_DEV + 1)
    return (start_out.astype(jnp.int32), end_out.astype(jnp.int32))


def draw_window_start(key, part):
    return window_bounds(key)[0]


def draw_window_end(key, part):
    return window_bounds(key)[1]


def block_scale(stream_key, dims, cuts, smallest, high):
    def one(dim, shards_of):
        heights = jax.random.uniform(jax.random.fold_in(jax.random.fold_in(stream_key, 6), dim), (shards_of,), jnp.float32, smallest / len(cuts), high / len(cuts))
        return jnp.repeat(jnp.exp(heights), dims[dim] // shards_of).reshape((-1,) + (1,) * (len(dims) - dim - 1))

    loudness = one(*cuts[0])
    for cut in cuts[1:]:
        loudness = loudness * one(*cut)
    return loudness


def normal_values(key, dims, scale, reach, pieces=(), kind=jnp.bfloat16):
    values = jax.random.normal(key, dims, jnp.float32) * scale
    if len(pieces) > 0:
        values = block_scale(key, dims, pieces, -0.22, 0.18) * values
    return jnp.clip(values, min=-reach, max=reach).astype(kind)


def setup_inputs(seed: int = 0) -> dict:
    keys = jax.random.split(jax.random.key(seed), 5)
    return {
        "genotypes": draw_genotypes(jax.random.fold_in(keys[4], 71), 0),
        "annotations": normal_values(keys[1], (SNPS, C), 0.0625, 0.3984375, ((0, 8),)),
        "window_start": draw_window_start(jax.random.fold_in(keys[4], 71), 0),
        "window_end": draw_window_end(jax.random.fold_in(keys[4], 71), 0),
    }


def adjust_block(gram_tile, row_sumsq, col_sumsq, col_ids, start_rows, end_rows, count_all):
    col_safe = jnp.where(col_sumsq > 0.0, col_sumsq, 1.0)
    corr_value = gram_tile * lax.rsqrt(row_sumsq)[:, None] * lax.rsqrt(col_safe)[None, :]
    squared = corr_value * corr_value
    adjusted = squared - (1.0 - squared) / (count_all - 2.0)
    inside = (col_ids[None, :] >= start_rows[:, None]) & (col_ids[None, :] < end_rows[:, None])
    return jnp.where(inside, adjusted, 0.0).astype(jnp.bfloat16)

def reference(genotypes, annotations, window_start, window_end):
    geno_pad = jnp.pad(genotypes, ((0, 0), (S_DEV, S_DEV)))
    annot_pad = jnp.pad(annotations, ((S_DEV, S_DEV), (0, 0)))
    count_all = float(IND)

    def one_stripe(stripe_id):
        row_first = (stripe_id * S_DEV).astype(jnp.int32)
        row_block = lax.dynamic_slice_in_dim(genotypes, row_first, S_DEV, 1).astype(jnp.float32)
        col_block = lax.dynamic_slice_in_dim(geno_pad, row_first, 3 * S_DEV, 1).astype(jnp.float32)
        gram_tile = jnp.dot(row_block.T, col_block, precision=lax.Precision.HIGHEST)
        col_sumsq = lax.optimization_barrier(jnp.sum(col_block * col_block, axis=0))
        row_sumsq = lax.optimization_barrier(jnp.sum(row_block * row_block, axis=0))
        col_ids = row_first - S_DEV + jnp.arange(3 * S_DEV, dtype=jnp.int32)
        start_rows = lax.dynamic_slice_in_dim(window_start, row_first, S_DEV, 0)
        end_rows = lax.dynamic_slice_in_dim(window_end, row_first, S_DEV, 0)
        weights = adjust_block(gram_tile, row_sumsq, col_sumsq, col_ids, start_rows, end_rows, count_all)
        annot_block = lax.dynamic_slice_in_dim(annot_pad, row_first, 3 * S_DEV, 0)
        return jnp.dot(weights, annot_block, preferred_element_type=jnp.float32)
    blocks = lax.map(one_stripe, jnp.arange(N_SNP, dtype=jnp.int32))
    return blocks.reshape(SNPS, C)
```

```python
import jax
import jax.numpy as jnp
from jax import lax
from jax.sharding import PartitionSpec as P


def shifted(array, axis, by):
    devices = lax.axis_size(axis)
    pairs = [(i, i + by) for i in range(devices) if 0 <= i + by < devices]
    return lax.ppermute(array, axis, pairs)


def ring(array, axis, by):
    devices = lax.axis_size(axis)
    return lax.ppermute(array, axis, [(i, (i + by) % devices) for i in range(devices)])


def after(value, *earlier):
    return lax.optimization_barrier((value, *earlier))[0]


def column_squares(block):
    widened = block.astype(jnp.float32)
    return jnp.sum(widened * widened, axis=0)


def transposed_product(left, right):
    return lax.dot_general(
        left, right, (((0,), (0,)), ((), ())), preferred_element_type=jnp.float32
    )


def summed_slots(slots, axis):
    devices = lax.axis_size(axis)
    place = lax.axis_index(axis)
    total = lax.dynamic_index_in_dim(slots, place, 0, keepdims=False).astype(jnp.float32)
    terms = []
    for by in range(1, devices):
        mine = lax.dynamic_index_in_dim(slots, (place + by) % devices, 0, keepdims=False)
        terms.append(ring(mine, axis, by))
    for term in terms:
        total = total + term.astype(jnp.float32)
    return total


def adjusted(corr, count_all):
    squared = corr * corr
    return (squared - (1.0 - squared) / (count_all - 2.0)).astype(jnp.bfloat16)


def per_device(genotypes, annotations, window_start, window_end):
    stripe = genotypes.shape[1]
    groups = lax.axis_size("ind")
    count_all = float(genotypes.shape[0] * groups)
    sub_rows = stripe // groups
    place = lax.axis_index("ind")
    stripe_first = lax.axis_index("snp") * stripe
    geno_above = shifted(genotypes, "snp", -1)

    squares = column_squares(genotypes)
    sumsq = squares
    for by in range(1, groups):
        sumsq = sumsq + ring(squares, "ind", by)
    unsafe = lax.rsqrt(sumsq)
    safe = lax.rsqrt(jnp.where(sumsq > 0.0, sumsq, 1.0))
    safe_above = shifted(safe, "snp", -1)

    own_part = transposed_product(genotypes, genotypes) * unsafe[:, None] * safe[None, :]
    own_part = own_part.astype(jnp.float16).reshape(groups, sub_rows, stripe)
    own_corr = summed_slots(own_part, "ind")

    cross_part = transposed_product(genotypes, geno_above) * safe[:, None] * safe_above[None, :]
    cross_part = cross_part.astype(jnp.float16).reshape(groups, sub_rows, groups, sub_rows)
    slots = jnp.stack([
        jnp.stack([cross_part[max(d, m), :, min(d, m), :] for m in range(groups)])
        for d in range(groups)
    ])
    cross_corr = summed_slots(slots, "ind")

    own_weights = adjusted(own_corr, count_all)
    cross_weights = adjusted(cross_corr, count_all)
    cross_below = shifted(cross_weights, "snp", 1)

    ids = jnp.arange(stripe, dtype=jnp.int32)
    own_ids = stripe_first + ids
    inside = (own_ids[None, :] >= window_start[:, None]) & (own_ids[None, :] < window_end[:, None])
    own_weights = jnp.where(inside, own_weights, 0)

    blocks = jnp.arange(groups, dtype=jnp.int32)
    above_ids = (own_ids + stripe).reshape(groups, 1, sub_rows)
    inside = (above_ids < window_end[None, :, None]) & (blocks <= place)[:, None, None]
    above_weights = jnp.where(inside, cross_weights, 0)
    below_ids = (own_ids - stripe).reshape(groups, sub_rows, 1)
    inside = (below_ids >= window_start[None, None, :]) & (blocks >= place)[:, None, None]
    below_weights = jnp.where(inside, cross_below, 0).reshape(stripe, sub_rows)

    later = after(annotations, geno_above)
    annot_above = shifted(later, "snp", -1).reshape(groups, sub_rows, -1)
    annot_below = shifted(later, "snp", 1)
    score = jnp.dot(own_weights, annotations, preferred_element_type=jnp.float32)
    score += lax.dot_general(
        above_weights, annot_above, (((0, 2), (0, 1)), ((), ())), preferred_element_type=jnp.float32
    )
    return score + transposed_product(below_weights, annot_below)


def solution(mesh):
    in_specs = (P("ind", "snp"), P("snp", None), P(("snp", "ind")), P(("snp", "ind")))
    out_specs = P(("snp", "ind"), None)
    return jax.shard_map(
        per_device, mesh=mesh, in_specs=in_specs, out_specs=out_specs, check_vma=False
    )
```

```python
import jax
import jax.numpy as jnp
from jax import lax
from jax.sharding import PartitionSpec as P


def shifted(array, axis, by):
    devices = lax.axis_size(axis)
    pairs = [(i, i + by) for i in range(devices) if 0 <= i + by < devices]
    return lax.ppermute(array, axis, pairs)


def ring(array, axis, by):
    devices = lax.axis_size(axis)
    return lax.ppermute(array, axis, [(i, (i + by) % devices) for i in range(devices)])


def after(value, *earlier):
    return lax.optimization_barrier((value, *earlier))[0]


def column_squares(block):
    widened = block.astype(jnp.float32)
    return jnp.sum(widened * widened, axis=0)


def transposed_product(left, right):
    return lax.dot_general(
        left, right, (((0,), (0,)), ((), ())), preferred_element_type=jnp.float32
    )


def exchanged(slots, axis):
    devices = lax.axis_size(axis)
    place = lax.axis_index(axis)
    mine = [
        lax.dynamic_index_in_dim(slots, (place + by) % devices, 0, keepdims=False)
        for by in range(devices)
    ]
    return [mine[0]] + [ring(mine[by], axis, by) for by in range(1, devices)]


def total(terms):
    result = terms[0].astype(jnp.float32)
    for term in terms[1:]:
        result = result + term.astype(jnp.float32)
    return result


def inverse_norm(sumsq):
    return lax.rsqrt(jnp.where(sumsq > 0.0, sumsq, 1.0))


def adjusted(corr, count_all):
    squared = corr * corr
    return (squared - (1.0 - squared) / (count_all - 2.0)).astype(jnp.bfloat16)


def per_device(genotypes, annotations, window_start, window_end):
    stripe = genotypes.shape[1]
    groups = lax.axis_size("ind")
    count_all = float(genotypes.shape[0] * groups)
    sub_rows = stripe // groups
    place = lax.axis_index("ind")
    stripe_first = lax.axis_index("snp") * stripe
    geno_above = shifted(genotypes, "snp", -1)

    squares = column_squares(genotypes)
    scale = inverse_norm(squares)
    own_part = transposed_product(genotypes, genotypes) * scale[:, None] * scale[None, :]
    own_part = own_part.astype(jnp.float16).reshape(groups, sub_rows, stripe)
    own_terms = exchanged(own_part, "ind")

    all_squares = [squares] + [ring(squares, "ind", by) for by in range(1, groups)]
    sumsq = total(all_squares)
    safe = inverse_norm(sumsq)
    safe_above = shifted(safe, "snp", -1)
    start_above = shifted(window_start, "snp", -1)

    geno_above = after(geno_above, *own_terms)
    cross_part = transposed_product(genotypes, geno_above) * safe[:, None] * safe_above[None, :]
    cross_part = cross_part.astype(jnp.float16).reshape(groups, sub_rows, groups, sub_rows)
    slots = jnp.stack([
        jnp.stack([cross_part[max(d, m), :, min(d, m), :] for m in range(groups)])
        for d in range(groups)
    ])
    cross_corr = total(exchanged(slots, "ind"))

    ids = jnp.arange(stripe, dtype=jnp.int32)
    own_ids = stripe_first + ids

    def rows_of(vector):
        return lax.dynamic_slice_in_dim(vector, place * sub_rows, sub_rows, 0)

    row_norm = lax.rsqrt(rows_of(sumsq))
    own_corr = 0.0
    for term, part in zip(own_terms, all_squares):
        norm = part * inverse_norm(part)
        row_factor = rows_of(norm) * row_norm
        own_corr += term.astype(jnp.float32) * row_factor[:, None] * (norm * safe)[None, :]
    inside = (own_ids[None, :] >= window_start[:, None]) & (own_ids[None, :] < window_end[:, None])
    own_weights = jnp.where(inside, adjusted(own_corr, count_all), 0)
    score = jnp.dot(own_weights, annotations, preferred_element_type=jnp.float32)

    cross_weights = adjusted(cross_corr, count_all)
    blocks = jnp.arange(groups, dtype=jnp.int32)
    row_ids = own_ids.reshape(groups, sub_rows, 1)
    inside = (row_ids >= start_above[None, None, :]) & (blocks >= place)[:, None, None]
    mirrored = jnp.where(inside, cross_weights, 0).reshape(stripe, sub_rows)
    mirrored = transposed_product(mirrored, annotations).astype(jnp.bfloat16)
    mirrored = shifted(mirrored, "snp", 1)

    above_ids = (own_ids + stripe).reshape(groups, 1, sub_rows)
    inside = (above_ids < window_end[None, :, None]) & (blocks <= place)[:, None, None]
    above_weights = jnp.where(inside, cross_weights, 0)
    annot_above = shifted(after(annotations, geno_above), "snp", -1).reshape(groups, sub_rows, -1)
    score += lax.dot_general(
        above_weights, annot_above, (((0, 2), (0, 1)), ((), ())), preferred_element_type=jnp.float32
    )
    return score + mirrored.astype(jnp.float32)


def solution(mesh):
    in_specs = (P("ind", "snp"), P("snp", None), P(("snp", "ind")), P(("snp", "ind")))
    out_specs = P(("snp", "ind"), None)
    return jax.shard_map(
        per_device, mesh=mesh, in_specs=in_specs, out_specs=out_specs, check_vma=False
    )
```

```python
import jax
import jax.numpy as jnp
from jax import lax
from jax.experimental import pallas as pl
from jax.experimental.pallas import tpu as pltpu
from jax.sharding import PartitionSpec as P


def shifted(array, axis, by):
    devices = lax.axis_size(axis)
    pairs = [(i, i + by) for i in range(devices) if 0 <= i + by < devices]
    return lax.ppermute(array, axis, pairs)


def ring(array, axis, by):
    devices = lax.axis_size(axis)
    return lax.ppermute(array, axis, [(i, (i + by) % devices) for i in range(devices)])


def after(value, *earlier):
    return lax.optimization_barrier((value, *earlier))[0]


def column_squares(block):
    widened = block.astype(jnp.float32)
    return jnp.sum(widened * widened, axis=0)


def transposed_product(left, right):
    return lax.dot_general(
        left, right, (((0,), (0,)), ((), ())), preferred_element_type=jnp.float32
    )


def exchanged(slots, axis, extra=None):
    devices = lax.axis_size(axis)
    place = lax.axis_index(axis)
    terms = []
    for by in range(devices):
        mine = lax.dynamic_index_in_dim(slots, (place + by) % devices, 0, keepdims=False)
        if extra is not None:
            mine = jnp.concatenate([mine, extra], axis=0)
        terms.append(mine if by == 0 else ring(mine, axis, by))
    return terms


def coded(norm):
    exponent = jnp.floor(jnp.log2(jnp.where(norm > 0.0, norm, 1.0)))
    mantissa = norm * jnp.exp2(-exponent)
    high = lax.optimization_barrier(mantissa.astype(jnp.float16))
    low = (mantissa - high.astype(jnp.float32)).astype(jnp.float16)
    rows = jnp.stack([high, low, exponent.astype(jnp.float16)])
    return jnp.pad(rows, ((0, 13), (0, 0)))


def decoded(rows):
    high, low, exponent = (rows[i].astype(jnp.float32) for i in range(3))
    return (high + low) * jnp.exp2(exponent)


def inverse_norm(sumsq):
    return lax.rsqrt(jnp.where(sumsq > 0.0, sumsq, 1.0))


def adjusted(corr, count_all):
    squared = corr * corr
    return (squared - (1.0 - squared) / (count_all - 2.0)).astype(jnp.bfloat16)


def completed_kernel(left, right, left_scale, right_scale, out):
    product = transposed_product(left[...], right[...])
    product = product * left_scale[...] * right_scale[...]
    rows = lax.broadcasted_iota(jnp.int32, product.shape, 0)
    columns = lax.broadcasted_iota(jnp.int32, product.shape, 1)
    out[...] = jnp.where(rows >= columns, product, product.T)


def completed_product(left, right, left_scale, right_scale):
    depth, width = left.shape
    return pl.pallas_call(
        completed_kernel,
        out_shape=jax.ShapeDtypeStruct((width, width), jnp.float32),
        compiler_params=pltpu.CompilerParams(vmem_limit_bytes=32 * 1024 * 1024),
        cost_estimate=pl.CostEstimate(
            flops=2 * depth * width * width, bytes_accessed=4 * depth * width, transcendentals=0
        ),
    )(left, right, left_scale[:, None], right_scale[None, :])


def per_device(genotypes, annotations, window_start, window_end):
    stripe = genotypes.shape[1]
    groups = lax.axis_size("ind")
    count_all = float(genotypes.shape[0] * groups)
    sub_rows = stripe // groups
    place = lax.axis_index("ind")
    stripe_first = lax.axis_index("snp") * stripe
    geno_above = shifted(genotypes, "snp", -1)

    squares = column_squares(genotypes)
    scale = inverse_norm(squares)
    own_part = transposed_product(genotypes, genotypes) * scale[:, None] * scale[None, :]
    own_part = own_part.astype(jnp.float16).reshape(groups, sub_rows, stripe)
    own_terms = exchanged(own_part, "ind", coded(squares * scale))

    first, second = own_terms[-1], own_terms[-2]
    scale_above = inverse_norm(shifted(after(squares, first), "snp", -1))
    annot_above = shifted(after(annotations, first, second), "snp", -1)

    geno_above = after(geno_above, first, second)
    cross_part = completed_product(genotypes, geno_above, scale, scale_above)
    cross_part = cross_part.astype(jnp.float16).reshape(groups, sub_rows, stripe)
    cross_terms = exchanged(cross_part, "ind")

    norms = jnp.stack([decoded(after(term[sub_rows:], cross_part)) for term in own_terms])
    sumsq = jnp.sum(norms * norms, axis=0)
    shares = norms * inverse_norm(sumsq)
    starts = jnp.pad(window_start.astype(jnp.float32), (0, stripe - sub_rows))
    above = shifted(jnp.concatenate([shares, starts[None]]), "snp", -1)
    shares_above = above[:groups]
    start_above = above[groups, :sub_rows].astype(jnp.int32)

    def rows_of(array):
        return lax.dynamic_slice_in_dim(array, place * sub_rows, sub_rows, array.ndim - 1)

    ids = jnp.arange(stripe, dtype=jnp.int32)
    own_ids = stripe_first + ids
    row_ids = place * sub_rows + jnp.arange(sub_rows, dtype=jnp.int32)
    lower = row_ids[:, None] >= ids[None, :]
    row_shares = rows_of(norms) * lax.rsqrt(rows_of(sumsq))
    row_safe = rows_of(shares)
    row_above = rows_of(shares_above)
    own_corr = 0.0
    cross_corr = 0.0
    for by in range(groups):
        own = own_terms[by][:sub_rows].astype(jnp.float32)
        own_corr += own * row_shares[by][:, None] * shares[by][None, :]
        cross = cross_terms[by].astype(jnp.float32)
        below = row_safe[by][:, None] * shares_above[by][None, :]
        cross_corr += cross * jnp.where(lower, below, row_above[by][:, None] * shares[by][None, :])

    inside = (own_ids[None, :] >= window_start[:, None]) & (own_ids[None, :] < window_end[:, None])
    own_weights = jnp.where(inside, adjusted(own_corr, count_all), 0)
    score = jnp.dot(own_weights, annotations, preferred_element_type=jnp.float32)

    cross_weights = adjusted(cross_corr, count_all)
    inside = (own_ids[None, :] >= start_above[:, None]) & (ids[None, :] >= row_ids[:, None])
    mirrored = jnp.where(inside, cross_weights, 0)
    mirrored = jnp.dot(mirrored, annotations, preferred_element_type=jnp.float32)
    mirrored = shifted(mirrored.astype(jnp.bfloat16), "snp", 1)

    inside = (own_ids[None, :] + stripe < window_end[:, None]) & lower
    above_weights = jnp.where(inside, cross_weights, 0)
    score += jnp.dot(above_weights, annot_above, preferred_element_type=jnp.float32)
    return score + mirrored.astype(jnp.float32)


def solution(mesh):
    in_specs = (P("ind", "snp"), P("snp", None), P(("snp", "ind")), P(("snp", "ind")))
    out_specs = P(("snp", "ind"), None)
    return jax.shard_map(
        per_device, mesh=mesh, in_specs=in_specs, out_specs=out_specs, check_vma=False
    )
```

```python
import functools

import jax
import jax.numpy as jnp
from jax import lax
from jax.experimental import pallas as pl
from jax.experimental.pallas import tpu as pltpu
from jax.sharding import PartitionSpec as P

UNIT = 32000.0
COST_T, COST_O, COST_F, COST_S, COST_H = 2.0, 2.5, 2.5, 2.0, 1.0
LANES = 128
CODE_ROWS = 16


def shifted(array, axis, by):
    devices = lax.axis_size(axis)
    pairs = [(i, i + by) for i in range(devices) if 0 <= i + by < devices]
    return lax.ppermute(array, axis, pairs)


def after(value, *earlier):
    return lax.optimization_barrier((value, *earlier))[0]


def exchanged(slabs, axis):
    devices = lax.axis_size(axis)
    return [slabs[0]] + [
        lax.ppermute(slabs[by], axis, [(i, i ^ by) for i in range(devices)])
        for by in range(1, devices)
    ]


def column_squares(block):
    widened = block.astype(jnp.float32)
    return jnp.sum(widened * widened, axis=0, keepdims=True)


def transposed_product(left, right):
    return lax.dot_general(
        left, right, (((0,), (0,)), ((), ())), preferred_element_type=jnp.float32
    )


def inverse_norm(sumsq):
    return lax.rsqrt(jnp.where(sumsq > 0.0, sumsq, 1.0))


def as_columns(row, width):
    return jnp.broadcast_to(row, (width, row.shape[1])).T


def mirrored_lower(square):
    rows = lax.broadcasted_iota(jnp.int32, square.shape, 0)
    columns = lax.broadcasted_iota(jnp.int32, square.shape, 1)
    return jnp.where(rows >= columns, square, square.T)


def to_fixed(values):
    return jnp.round(values * UNIT).astype(jnp.int32).astype(jnp.int16)


def coded(norm):
    exponent = jnp.floor(jnp.log2(jnp.where(norm > 0.0, norm, 1.0)))
    mantissa = norm * jnp.exp2(-exponent) * 8192.0
    high = jnp.floor(mantissa)
    low = jnp.floor((mantissa - high) * 16384.0 + 0.5)
    rows = lax.broadcasted_iota(jnp.int32, (CODE_ROWS, norm.shape[1]), 0)
    values = jnp.where(rows == 0, high, jnp.where(rows == 1, low, exponent))
    return jnp.where(rows < 3, values, 0.0).astype(jnp.int32).astype(jnp.int16)


def decoded(rows):
    rows = rows.astype(jnp.int32).astype(jnp.float32)
    mantissa = (rows[0:1] + rows[1:2] * (1.0 / 16384.0)) * (1.0 / 8192.0)
    return mantissa * jnp.exp2(rows[2:3])


def adjusted(corr, count_all):
    squared = corr * corr
    return squared - (1.0 - squared) / (count_all - 2.0)


def kernel_call(kernel, out_shape, operands, in_specs=None, grid=None, scratch=(), cost=0.0):
    in_specs = in_specs or [None] * len(operands)
    whole = pl.BlockSpec(memory_space=pltpu.VMEM)
    extra = {} if grid is None else {"grid": grid}
    return pl.pallas_call(
        kernel,
        out_shape=out_shape,
        in_specs=[spec or whole for spec in in_specs],
        scratch_shapes=list(scratch),
        compiler_params=pltpu.CompilerParams(vmem_limit_bytes=36 * 1024 * 1024),
        cost_estimate=pl.CostEstimate(flops=0, bytes_accessed=int(cost * 3.7e6), transcendentals=0),
        **extra,
    )(*operands)


def write_slabs(place, values, slabs):
    rows = values.shape[0] // len(slabs)
    for by, slab in enumerate(slabs):
        first = (place ^ by) * rows
        slab[:rows] = to_fixed(values[pl.ds(pl.multiple_of(first, 16), rows), :])


def own_kernel(groups, place, array, second, scale, *rest):
    slabs, values = rest[:groups], rest[groups]
    second[...] = array[:, second.shape[1] :]
    squares = column_squares(array[...])
    inverse = inverse_norm(squares)
    scale[...] = inverse
    product = transposed_product(array[...], array[...])
    columns = as_columns(inverse, LANES)
    columns = jnp.concatenate([columns] * (product.shape[1] // LANES), axis=1)
    values[...] = product * columns * inverse
    write_slabs(place[0], values, slabs)
    code = coded(squares * inverse)
    for slab in slabs:
        slab[-CODE_ROWS:] = code


def scaled_product(left, right, left_scale):
    right_scale = inverse_norm(column_squares(right))
    product = transposed_product(left, right)
    columns = as_columns(left_scale, LANES)
    columns = jnp.concatenate([columns] * (product.shape[1] // LANES), axis=1)
    return product * columns * right_scale


def first_kernel(groups, place, left, right, left_scale, corner, *rest):
    slabs, values = rest[:groups], rest[groups]
    half = right.shape[1]
    product = scaled_product(left[...], right[...], left_scale[...])
    values[:half] = mirrored_lower(product[:half])
    values[half:] = product[half:]
    corner[...] = product[half:]
    write_slabs(place[0], values, slabs)


def second_kernel(groups, place, left, right, left_scale, corner, *rest):
    slabs, values = rest[:groups], rest[groups]
    half = right.shape[1]
    values[:half] = corner[...].T
    values[half:] = mirrored_lower(scaled_product(left[...], right[...], left_scale[...]))
    write_slabs(place[0], values, slabs)


def shares_kernel(groups, starts, *rest):
    terms, (rows, columns) = rest[:groups], rest[groups:]
    norms = [decoded(term[...]) for term in terms]
    sumsq = functools.reduce(jnp.add, [norm * norm for norm in norms])
    inverse = inverse_norm(sumsq)
    rows[...] = jnp.zeros(rows.shape, jnp.float32)
    for by, norm in enumerate(norms):
        rows[by : by + 1, :] = norm * inverse
    rows[groups : groups + 1, : starts.shape[1]] = starts[...].astype(jnp.float32)
    rows[groups + 1 : groups + 2, :] = sumsq * lax.rsqrt(sumsq) * inverse
    fill = jnp.zeros((LANES - rows.shape[0], rows.shape[1]), jnp.float32)
    columns[...] = jnp.concatenate([rows[...], fill], axis=0).T


def per_device(genotypes, annotations, window_start, window_end):
    stripe = genotypes.shape[1]
    half = stripe // 2
    groups = lax.axis_size("ind")
    count_all = float(genotypes.shape[0] * groups)
    sub_rows = stripe // groups
    place = lax.axis_index("ind").astype(jnp.int32)
    place = jnp.stack([place, lax.axis_index("snp").astype(jnp.int32) * stripe])
    scalar = pl.BlockSpec(memory_space=pltpu.SMEM)

    def shape(*dims, dtype=jnp.float32):
        return jax.ShapeDtypeStruct(dims, dtype)

    def slab_shapes(rows, columns):
        return (shape(rows, columns, dtype=jnp.int16),) * groups

    above_first = shifted(genotypes[:, :half], "snp", -1)
    second, scale, *own_slabs = kernel_call(
        functools.partial(own_kernel, groups),
        (
            shape(genotypes.shape[0], half, dtype=genotypes.dtype),
            shape(1, stripe),
            *slab_shapes(sub_rows + CODE_ROWS, stripe),
        ),
        (place, genotypes),
        [scalar, None],
        scratch=[pltpu.VMEM((stripe, stripe), jnp.float32)],
        cost=COST_O,
    )
    own_terms = exchanged(own_slabs, "ind")
    above_second = shifted(second, "snp", -1)

    above_first = after(above_first, own_terms[1])
    corner, *first_slabs = kernel_call(
        functools.partial(first_kernel, groups),
        (shape(half, half), *slab_shapes(sub_rows, half)),
        (place, genotypes, above_first, scale),
        [scalar, None, None, None],
        scratch=[pltpu.VMEM((stripe, half), jnp.float32)],
        cost=COST_F,
    )
    first_terms = exchanged(first_slabs, "ind")
    annot_above = shifted(after(annotations, own_terms[1]), "snp", -1)

    above_second = after(above_second, first_terms[1])
    second_slabs = kernel_call(
        functools.partial(second_kernel, groups),
        slab_shapes(sub_rows, half),
        (place, genotypes, above_second, scale, corner),
        [
            scalar,
            pl.BlockSpec((genotypes.shape[0], half), lambda i: (0, 1)),
            None,
            pl.BlockSpec((1, half), lambda i: (0, 1)),
            None,
        ],
        grid=(1,),
        scratch=[pltpu.VMEM((stripe, half), jnp.float32)],
        cost=COST_S,
    )
    second_terms = exchanged(second_slabs, "ind")

    code = pl.BlockSpec((CODE_ROWS, stripe), lambda i: (sub_rows // CODE_ROWS, 0))
    info_rows = -(-(groups + 2) // 8) * 8
    shares, share_columns = kernel_call(
        functools.partial(shares_kernel, groups),
        (shape(info_rows, stripe), shape(stripe, LANES)),
        (window_start[None], *(after(term, corner) for term in own_terms)),
        [None] + [code] * groups,
        grid=(1,),
        cost=COST_H,
    )
    above = shifted(shares, "snp", -1)

    def rows_of(array):
        return lax.dynamic_slice_in_dim(array, place[0] * sub_rows, sub_rows, 0)

    ids = jnp.arange(stripe, dtype=jnp.int32)[None, :]
    row_ids = place[0] * sub_rows + jnp.arange(sub_rows, dtype=jnp.int32)[:, None]
    lower = row_ids >= ids
    own_ids = place[1] + ids
    here = rows_of(share_columns)
    next_here = rows_of(above.T)

    def column(array, by):
        return array[:, by : by + 1]

    def row(array, by):
        return array[by : by + 1, :]

    own_corr = sum(
        term[:sub_rows].astype(jnp.float32) * column(here, by) * row(shares, by)
        for by, term in enumerate(own_terms)
    )
    own_corr = own_corr * (1.0 / UNIT) * column(here, groups + 1)
    inside = (own_ids >= window_start[:, None]) & (own_ids < window_end[:, None])
    own_weights = jnp.where(inside, adjusted(own_corr, count_all), 0.0).astype(jnp.bfloat16)
    score = jnp.dot(own_weights, annotations, preferred_element_type=jnp.float32)

    cross_corr = 0.0
    for by in range(groups):
        term = jnp.concatenate([first_terms[by], second_terms[by]], axis=1).astype(jnp.float32)
        below = column(here, by) * row(above, by)
        cross_corr += term * jnp.where(lower, below, column(next_here, by) * row(shares, by))
    cross_weights = adjusted(cross_corr * (1.0 / UNIT), count_all).astype(jnp.bfloat16)
    start_above = above[groups, :sub_rows].astype(jnp.int32)
    inside = (own_ids >= start_above[:, None]) & (ids >= row_ids)
    mirrored = jnp.where(inside, cross_weights, 0)
    mirrored = jnp.dot(mirrored, annotations, preferred_element_type=jnp.float32)
    mirrored = shifted(mirrored.astype(jnp.bfloat16), "snp", 1)

    inside = (own_ids + stripe < window_end[:, None]) & lower
    above_weights = jnp.where(inside, cross_weights, 0)
    score += jnp.dot(above_weights, annot_above, preferred_element_type=jnp.float32)
    return score + mirrored.astype(jnp.float32)


def solution(mesh):
    in_specs = (P("ind", "snp"), P("snp", None), P(("snp", "ind")), P(("snp", "ind")))
    out_specs = P(("snp", "ind"), None)
    return jax.shard_map(
        per_device, mesh=mesh, in_specs=in_specs, out_specs=out_specs, check_vma=False
    )
```

```python
import functools

import jax
import jax.numpy as jnp
from jax import lax
from jax.experimental import pallas as pl
from jax.experimental.pallas import tpu as pltpu
from jax.sharding import PartitionSpec as P

UNIT = 32000.0
COST_T, COST_O, COST_F, COST_S, COST_H = 2.0, 2.5, 2.5, 2.0, 1.0
LANES = 128
CODE_ROWS = 16


def shifted(array, axis, by):
    devices = lax.axis_size(axis)
    pairs = [(i, i + by) for i in range(devices) if 0 <= i + by < devices]
    return lax.ppermute(array, axis, pairs)


def after(value, *earlier):
    return lax.optimization_barrier((value, *earlier))[0]


def exchanged(slabs, axis):
    devices = lax.axis_size(axis)
    terms = [slabs[0]] * devices
    for by in range(1, devices):
        pairs = [(i, (i + by) % devices) for i in range(devices)]
        terms[by] = lax.ppermute(slabs[by], axis, pairs)
    return terms


def column_squares(block):
    widened = block.astype(jnp.float32)
    return jnp.sum(widened * widened, axis=0, keepdims=True)


def transposed_product(left, right):
    return lax.dot_general(
        left, right, (((0,), (0,)), ((), ())), preferred_element_type=jnp.float32
    )


def inverse_norm(sumsq):
    return lax.rsqrt(jnp.where(sumsq > 0.0, sumsq, 1.0))


def as_columns(row, width):
    return jnp.broadcast_to(row, (width, row.shape[1])).T


def mirrored_lower(square):
    rows = lax.broadcasted_iota(jnp.int32, square.shape, 0)
    columns = lax.broadcasted_iota(jnp.int32, square.shape, 1)
    return jnp.where(rows >= columns, square, square.T)


def to_fixed(values):
    return jnp.round(values * UNIT).astype(jnp.int32).astype(jnp.int16)


def coded(norm):
    exponent = jnp.floor(jnp.log2(jnp.where(norm > 0.0, norm, 1.0)))
    mantissa = norm * jnp.exp2(-exponent) * 8192.0
    high = jnp.floor(mantissa)
    low = jnp.floor((mantissa - high) * 16384.0 + 0.5)
    rows = lax.broadcasted_iota(jnp.int32, (CODE_ROWS, norm.shape[1]), 0)
    values = jnp.where(rows == 0, high, jnp.where(rows == 1, low, exponent))
    return jnp.where(rows < 3, values, 0.0).astype(jnp.int32).astype(jnp.int16)


def decoded(rows):
    rows = rows.astype(jnp.int32).astype(jnp.float32)
    mantissa = (rows[0:1] + rows[1:2] * (1.0 / 16384.0)) * (1.0 / 8192.0)
    return mantissa * jnp.exp2(rows[2:3])


def adjusted(corr, count_all):
    squared = corr * corr
    return squared - (1.0 - squared) / (count_all - 2.0)


def kernel_call(kernel, out_shape, operands, in_specs=None, grid=None, scratch=(), cost=0.0):
    in_specs = in_specs or [None] * len(operands)
    whole = pl.BlockSpec(memory_space=pltpu.VMEM)
    extra = {} if grid is None else {"grid": grid}
    return pl.pallas_call(
        kernel,
        out_shape=out_shape,
        in_specs=[spec or whole for spec in in_specs],
        scratch_shapes=list(scratch),
        compiler_params=pltpu.CompilerParams(vmem_limit_bytes=36 * 1024 * 1024),
        cost_estimate=pl.CostEstimate(flops=0, bytes_accessed=int(cost * 3.7e6), transcendentals=0),
        **extra,
    )(*operands)


def write_slabs(place, values, slabs):
    rows = values.shape[0] // len(slabs)
    for by, slab in enumerate(slabs):
        first = lax.rem(place + by, len(slabs)) * rows
        slab[:rows] = to_fixed(values[pl.ds(pl.multiple_of(first, 16), rows), :])


def own_kernel(groups, place, array, second, scale, *rest):
    slabs, values = rest[:groups], rest[groups]
    second[...] = array[:, second.shape[1] :]
    squares = column_squares(array[...])
    inverse = inverse_norm(squares)
    scale[...] = inverse
    product = transposed_product(array[...], array[...])
    columns = as_columns(inverse, LANES)
    columns = jnp.concatenate([columns] * (product.shape[1] // LANES), axis=1)
    values[...] = product * columns * inverse
    write_slabs(place[0], values, slabs)
    code = coded(squares * inverse)
    for slab in slabs:
        slab[-CODE_ROWS:] = code


def scaled_product(left, right, left_scale):
    right_scale = inverse_norm(column_squares(right))
    product = transposed_product(left, right)
    columns = as_columns(left_scale, LANES)
    columns = jnp.concatenate([columns] * (product.shape[1] // LANES), axis=1)
    return product * columns * right_scale


def first_kernel(groups, place, left, right, left_scale, corner, *rest):
    slabs, values = rest[:groups], rest[groups]
    half = right.shape[1]
    product = scaled_product(left[...], right[...], left_scale[...])
    values[:half] = mirrored_lower(product[:half])
    values[half:] = product[half:]
    corner[...] = product[half:]
    write_slabs(place[0], values, slabs)


def second_kernel(groups, place, left, right, left_scale, corner, *rest):
    slabs, values = rest[:groups], rest[groups]
    half = right.shape[1]
    values[:half] = corner[...].T
    values[half:] = mirrored_lower(scaled_product(left[...], right[...], left_scale[...]))
    write_slabs(place[0], values, slabs)


def shares_kernel(groups, starts, *rest):
    terms, (rows, columns) = rest[:groups], rest[groups:]
    norms = [decoded(term[...]) for term in terms]
    sumsq = functools.reduce(jnp.add, [norm * norm for norm in norms])
    inverse = inverse_norm(sumsq)
    rows[...] = jnp.zeros(rows.shape, jnp.float32)
    for by, norm in enumerate(norms):
        rows[by : by + 1, :] = norm * inverse
    rows[groups : groups + 1, : starts.shape[1]] = starts[...].astype(jnp.float32)
    rows[groups + 1 : groups + 2, :] = sumsq * lax.rsqrt(sumsq) * inverse
    fill = jnp.zeros((LANES - rows.shape[0], rows.shape[1]), jnp.float32)
    columns[...] = jnp.concatenate([rows[...], fill], axis=0).T


def per_device(genotypes, annotations, window_start, window_end):
    stripe = genotypes.shape[1]
    half = stripe // 2
    groups = lax.axis_size("ind")
    count_all = float(genotypes.shape[0] * groups)
    sub_rows = stripe // groups
    place = lax.axis_index("ind").astype(jnp.int32)
    place = jnp.stack([place, lax.axis_index("snp").astype(jnp.int32) * stripe])
    scalar = pl.BlockSpec(memory_space=pltpu.SMEM)

    def shape(*dims, dtype=jnp.float32):
        return jax.ShapeDtypeStruct(dims, dtype)

    def slab_shapes(rows, columns):
        return (shape(rows, columns, dtype=jnp.int16),) * groups

    above_first = shifted(genotypes[:, :half], "snp", -1)
    second, scale, *own_slabs = kernel_call(
        functools.partial(own_kernel, groups),
        (
            shape(genotypes.shape[0], half, dtype=genotypes.dtype),
            shape(1, stripe),
            *slab_shapes(sub_rows + CODE_ROWS, stripe),
        ),
        (place, genotypes),
        [scalar, None],
        scratch=[pltpu.VMEM((stripe, stripe), jnp.float32)],
        cost=COST_O,
    )
    own_terms = exchanged(own_slabs, "ind")
    above_second = shifted(after(second, scale), "snp", -1)

    corner, *first_slabs = kernel_call(
        functools.partial(first_kernel, groups),
        (shape(half, half), *slab_shapes(sub_rows, half)),
        (place, genotypes, above_first, scale),
        [scalar, None, None, None],
        scratch=[pltpu.VMEM((stripe, half), jnp.float32)],
        cost=COST_F,
    )
    first_terms = exchanged([after(slab, own_terms[2]) for slab in first_slabs], "ind")
    annot_above = shifted(after(annotations, own_terms[1]), "snp", -1)

    code = pl.BlockSpec((CODE_ROWS, stripe), lambda i: (sub_rows // CODE_ROWS, 0))
    info_rows = -(-(groups + 2) // 8) * 8
    shares, share_columns = kernel_call(
        functools.partial(shares_kernel, groups),
        (shape(info_rows, stripe), shape(stripe, LANES)),
        (window_start[None], *(after(term, corner) for term in own_terms)),
        [None] + [code] * groups,
        grid=(1,),
        cost=COST_H,
    )
    above = shifted(shares, "snp", -1)

    above_second = after(above_second, first_terms[1])
    second_slabs = kernel_call(
        functools.partial(second_kernel, groups),
        slab_shapes(sub_rows, half),
        (place, genotypes, above_second, scale, corner),
        [
            scalar,
            pl.BlockSpec((genotypes.shape[0], half), lambda i: (0, 1)),
            None,
            pl.BlockSpec((1, half), lambda i: (0, 1)),
            None,
        ],
        grid=(1,),
        scratch=[pltpu.VMEM((stripe, half), jnp.float32)],
        cost=COST_S,
    )
    second_terms = exchanged(second_slabs, "ind")

    def rows_of(array):
        return lax.dynamic_slice_in_dim(array, place[0] * sub_rows, sub_rows, 0)

    ids = jnp.arange(stripe, dtype=jnp.int32)[None, :]
    row_ids = place[0] * sub_rows + jnp.arange(sub_rows, dtype=jnp.int32)[:, None]
    lower = row_ids >= ids
    own_ids = place[1] + ids
    here = rows_of(share_columns)
    next_here = rows_of(above.T)

    def column(array, by):
        return array[:, by : by + 1]

    def row(array, by):
        return array[by : by + 1, :]

    own_corr = sum(
        term[:sub_rows].astype(jnp.float32) * column(here, by) * row(shares, by)
        for by, term in enumerate(own_terms)
    )
    own_corr = own_corr * (1.0 / UNIT) * column(here, groups + 1)
    inside = (own_ids >= window_start[:, None]) & (own_ids < window_end[:, None])
    own_weights = jnp.where(inside, adjusted(own_corr, count_all), 0.0).astype(jnp.bfloat16)
    score = jnp.dot(own_weights, annotations, preferred_element_type=jnp.float32)

    cross_corr = 0.0
    for by in range(groups):
        term = jnp.concatenate([first_terms[by], second_terms[by]], axis=1).astype(jnp.float32)
        below = column(here, by) * row(above, by)
        cross_corr += term * jnp.where(lower, below, column(next_here, by) * row(shares, by))
    cross_weights = adjusted(cross_corr * (1.0 / UNIT), count_all).astype(jnp.bfloat16)
    start_above = above[groups, :sub_rows].astype(jnp.int32)
    inside = (own_ids >= start_above[:, None]) & (ids >= row_ids)
    mirrored = jnp.where(inside, cross_weights, 0)
    mirrored = jnp.dot(mirrored, annotations, preferred_element_type=jnp.float32)
    mirrored = shifted(mirrored.astype(jnp.bfloat16), "snp", 1)

    inside = (own_ids + stripe < window_end[:, None]) & lower
    above_weights = jnp.where(inside, cross_weights, 0)
    score += jnp.dot(above_weights, annot_above, preferred_element_type=jnp.float32)
    return score + mirrored.astype(jnp.float32)


def solution(mesh):
    in_specs = (P("ind", "snp"), P("snp", None), P(("snp", "ind")), P(("snp", "ind")))
    out_specs = P(("snp", "ind"), None)
    return jax.shard_map(
        per_device, mesh=mesh, in_specs=in_specs, out_specs=out_specs, check_vma=False
    )
```

```python
import functools

import jax
import jax.numpy as jnp
from jax import lax
from jax.experimental import pallas as pl
from jax.experimental.pallas import tpu as pltpu
from jax.sharding import PartitionSpec as P

UNIT = 32000.0
COST_T, COST_O, COST_F, COST_S, COST_H = 2.0, 2.5, 2.5, 2.0, 1.0
LANES = 128
CODE_ROWS = 8


def shifted(array, axis, by):
    devices = lax.axis_size(axis)
    pairs = [(i, i + by) for i in range(devices) if 0 <= i + by < devices]
    return lax.ppermute(array, axis, pairs)


def after(value, *earlier):
    return lax.optimization_barrier((value, *earlier))[0]


def exchanged(slabs, axis):
    devices = lax.axis_size(axis)
    terms = [slabs[0]] * devices
    for by in range(1, devices):
        pairs = [(i, (i + by) % devices) for i in range(devices)]
        terms[by] = lax.ppermute(slabs[by], axis, pairs)
    return terms


def column_squares(block):
    widened = block.astype(jnp.float32)
    return jnp.sum(widened * widened, axis=0, keepdims=True)


def transposed_product(left, right):
    return lax.dot_general(
        left, right, (((0,), (0,)), ((), ())), preferred_element_type=jnp.float32
    )


def inverse_norm(sumsq):
    return lax.rsqrt(jnp.where(sumsq > 0.0, sumsq, 1.0))


def as_columns(row, width):
    return jnp.broadcast_to(row, (width, row.shape[1])).T


def mirrored_lower(square):
    rows = lax.broadcasted_iota(jnp.int32, square.shape, 0)
    columns = lax.broadcasted_iota(jnp.int32, square.shape, 1)
    return jnp.where(rows >= columns, square, square.T)


def to_fixed(values):
    return jnp.round(values * UNIT).astype(jnp.int32).astype(jnp.int16)


def coded(norm):
    exponent = jnp.floor(jnp.log2(jnp.where(norm > 0.0, norm, 1.0)))
    mantissa = norm * jnp.exp2(-exponent) * 8192.0
    high = jnp.floor(mantissa)
    low = jnp.floor((mantissa - high) * 16384.0 + 0.5)
    rows = lax.broadcasted_iota(jnp.int32, (CODE_ROWS, norm.shape[1]), 0)
    values = jnp.where(rows == 0, high, jnp.where(rows == 1, low, exponent))
    return jnp.where(rows < 3, values, 0.0).astype(jnp.int32).astype(jnp.int16)


def decoded(rows):
    rows = rows.astype(jnp.int32).astype(jnp.float32)
    mantissa = (rows[0:1] + rows[1:2] * (1.0 / 16384.0)) * (1.0 / 8192.0)
    return mantissa * jnp.exp2(rows[2:3])


def adjusted(corr, count_all):
    squared = corr * corr
    return squared - (1.0 - squared) / (count_all - 2.0)


def kernel_call(kernel, out_shape, operands, in_specs=None, grid=None, scratch=(), cost=0.0):
    in_specs = in_specs or [None] * len(operands)
    whole = pl.BlockSpec(memory_space=pltpu.VMEM)
    extra = {} if grid is None else {"grid": grid}
    return pl.pallas_call(
        kernel,
        out_shape=out_shape,
        in_specs=[spec or whole for spec in in_specs],
        scratch_shapes=list(scratch),
        compiler_params=pltpu.CompilerParams(vmem_limit_bytes=36 * 1024 * 1024),
        cost_estimate=pl.CostEstimate(flops=0, bytes_accessed=int(cost * 3.7e6), transcendentals=0),
        **extra,
    )(*operands)


def write_slabs(place, values, slabs):
    rows = values.shape[0] // len(slabs)
    for by, slab in enumerate(slabs):
        first = lax.rem(place + by, len(slabs)) * rows
        slab[:rows] = to_fixed(values[pl.ds(pl.multiple_of(first, 16), rows), :])


def own_kernel(groups, place, array, second, scale, *rest):
    slabs, values = rest[:groups], rest[groups]
    second[...] = array[:, second.shape[1] :]
    squares = column_squares(array[...])
    inverse = inverse_norm(squares)
    scale[...] = inverse
    product = transposed_product(array[...], array[...])
    columns = as_columns(inverse, LANES)
    columns = jnp.concatenate([columns] * (product.shape[1] // LANES), axis=1)
    values[...] = product * columns * inverse
    write_slabs(place[0], values, slabs)
    code = coded(squares * inverse)
    for slab in slabs:
        slab[-CODE_ROWS:] = code


def scaled_product(left, right, left_scale):
    right_scale = inverse_norm(column_squares(right))
    product = transposed_product(left, right)
    columns = as_columns(left_scale, LANES)
    columns = jnp.concatenate([columns] * (product.shape[1] // LANES), axis=1)
    return product * columns * right_scale


def first_kernel(groups, place, left, right, left_scale, corner, *rest):
    slabs, values = rest[:groups], rest[groups]
    half = right.shape[1]
    product = scaled_product(left[...], right[...], left_scale[...])
    values[:half] = mirrored_lower(product[:half])
    values[half:] = product[half:]
    corner[...] = product[half:]
    write_slabs(place[0], values, slabs)


def second_kernel(groups, place, left, right, left_scale, corner, *rest):
    slabs, values = rest[:groups], rest[groups]
    half = right.shape[1]
    values[:half] = corner[...].T
    values[half:] = mirrored_lower(scaled_product(left[...], right[...], left_scale[...]))
    write_slabs(place[0], values, slabs)


def shares_kernel(groups, starts, *rest):
    terms, (rows, columns) = rest[:groups], rest[groups:]
    norms = [decoded(term[...]) for term in terms]
    sumsq = functools.reduce(jnp.add, [norm * norm for norm in norms])
    inverse = inverse_norm(sumsq)
    rows[...] = jnp.zeros(rows.shape, jnp.float32)
    for by, norm in enumerate(norms):
        rows[by : by + 1, :] = norm * inverse
    rows[groups : groups + 1, : starts.shape[1]] = starts[...].astype(jnp.float32)
    rows[groups + 1 : groups + 2, :] = sumsq * lax.rsqrt(sumsq) * inverse
    fill = jnp.zeros((LANES - rows.shape[0], rows.shape[1]), jnp.float32)
    columns[...] = jnp.concatenate([rows[...], fill], axis=0).T


def per_device(genotypes, annotations, window_start, window_end):
    stripe = genotypes.shape[1]
    half = stripe // 2
    groups = lax.axis_size("ind")
    count_all = float(genotypes.shape[0] * groups)
    sub_rows = stripe // groups
    place = lax.axis_index("ind").astype(jnp.int32)
    place = jnp.stack([place, lax.axis_index("snp").astype(jnp.int32) * stripe])
    scalar = pl.BlockSpec(memory_space=pltpu.SMEM)

    def shape(*dims, dtype=jnp.float32):
        return jax.ShapeDtypeStruct(dims, dtype)

    def slab_shapes(rows, columns):
        return (shape(rows, columns, dtype=jnp.int16),) * groups

    above_first = shifted(genotypes[:, :half], "snp", -1)
    second, scale, *own_slabs = kernel_call(
        functools.partial(own_kernel, groups),
        (
            shape(genotypes.shape[0], half, dtype=genotypes.dtype),
            shape(1, stripe),
            *slab_shapes(sub_rows + CODE_ROWS, stripe),
        ),
        (place, genotypes),
        [scalar, None],
        scratch=[pltpu.VMEM((stripe, stripe), jnp.float32)],
        cost=COST_O,
    )
    own_terms = exchanged(own_slabs, "ind")
    above_second = shifted(after(second, scale), "snp", -1)

    corner, *first_slabs = kernel_call(
        functools.partial(first_kernel, groups),
        (shape(half, half), *slab_shapes(sub_rows, half)),
        (place, genotypes, above_first, scale),
        [scalar, None, None, None],
        scratch=[pltpu.VMEM((stripe, half), jnp.float32)],
        cost=COST_F,
    )
    first_terms = exchanged([after(slab, own_terms[2]) for slab in first_slabs], "ind")
    annot_above = shifted(after(annotations, own_terms[1]), "snp", -1)

    code = pl.BlockSpec((CODE_ROWS, stripe), lambda i: (sub_rows // CODE_ROWS, 0))
    info_rows = -(-(groups + 2) // 8) * 8
    shares, share_columns = kernel_call(
        functools.partial(shares_kernel, groups),
        (shape(info_rows, stripe), shape(stripe, LANES)),
        (window_start[None], *(after(term, corner) for term in own_terms)),
        [None] + [code] * groups,
        grid=(1,),
        cost=COST_H,
    )
    above = shifted(shares, "snp", -1)

    above_second = after(above_second, first_terms[1])
    second_slabs = kernel_call(
        functools.partial(second_kernel, groups),
        slab_shapes(sub_rows, half),
        (place, genotypes, above_second, scale, corner),
        [
            scalar,
            pl.BlockSpec((genotypes.shape[0], half), lambda i: (0, 1)),
            None,
            pl.BlockSpec((1, half), lambda i: (0, 1)),
            None,
        ],
        grid=(1,),
        scratch=[pltpu.VMEM((stripe, half), jnp.float32)],
        cost=COST_S,
    )
    second_terms = exchanged(second_slabs, "ind")

    def rows_of(array):
        return lax.dynamic_slice_in_dim(array, place[0] * sub_rows, sub_rows, 0)

    ids = jnp.arange(stripe, dtype=jnp.int32)[None, :]
    row_ids = place[0] * sub_rows + jnp.arange(sub_rows, dtype=jnp.int32)[:, None]
    lower = row_ids >= ids
    own_ids = place[1] + ids
    here = rows_of(share_columns)
    next_here = rows_of(above.T)

    def column(array, by):
        return array[:, by : by + 1]

    def row(array, by):
        return array[by : by + 1, :]

    own_corr = sum(
        term[:sub_rows].astype(jnp.float32) * column(here, by) * row(shares, by)
        for by, term in enumerate(own_terms)
    )
    own_corr = own_corr * (1.0 / UNIT) * column(here, groups + 1)
    inside = (own_ids >= window_start[:, None]) & (own_ids < window_end[:, None])
    own_weights = jnp.where(inside, adjusted(own_corr, count_all), 0.0).astype(jnp.bfloat16)
    score = jnp.dot(own_weights, annotations, preferred_element_type=jnp.float32)

    cross_corr = 0.0
    for by in range(groups):
        term = jnp.concatenate([first_terms[by], second_terms[by]], axis=1).astype(jnp.float32)
        below = column(here, by) * row(above, by)
        cross_corr += term * jnp.where(lower, below, column(next_here, by) * row(shares, by))
    cross_weights = adjusted(cross_corr * (1.0 / UNIT), count_all).astype(jnp.bfloat16)
    start_above = above[groups, :sub_rows].astype(jnp.int32)
    inside = (own_ids >= start_above[:, None]) & (ids >= row_ids)
    mirrored = jnp.where(inside, cross_weights, 0)
    mirrored = jnp.dot(mirrored, annotations, preferred_element_type=jnp.float32)
    mirrored = shifted(mirrored.astype(jnp.bfloat16), "snp", 1)

    inside = (own_ids + stripe < window_end[:, None]) & lower
    above_weights = jnp.where(inside, cross_weights, 0)
    score += jnp.dot(above_weights, annot_above, preferred_element_type=jnp.float32)
    return score + mirrored.astype(jnp.float32)


def solution(mesh):
    in_specs = (P("ind", "snp"), P("snp", None), P(("snp", "ind")), P(("snp", "ind")))
    out_specs = P(("snp", "ind"), None)
    return jax.shard_map(
        per_device, mesh=mesh, in_specs=in_specs, out_specs=out_specs, check_vma=False
    )
```

```python
import functools

import jax
import jax.numpy as jnp
from jax import lax
from jax.experimental import pallas as pl
from jax.experimental.pallas import tpu as pltpu
from jax.sharding import PartitionSpec as P

UNIT = 32000.0
LANES = 128
CODE_ROWS = 8


def shifted(array, axis, by):
    devices = lax.axis_size(axis)
    pairs = [(i, i + by) for i in range(devices) if 0 <= i + by < devices]
    return lax.ppermute(array, axis, pairs)


def after(value, *earlier):
    return lax.optimization_barrier((value, *earlier))[0]


def exchanged(slabs, axis):
    devices = lax.axis_size(axis)
    terms = [slabs[0]] * devices
    for by in range(1, devices):
        pairs = [(i, (i + by) % devices) for i in range(devices)]
        terms[by] = lax.ppermute(slabs[by], axis, pairs)
    return terms


def column_squares(block):
    widened = block.astype(jnp.float32)
    return jnp.sum(widened * widened, axis=0, keepdims=True)


def transposed_product(left, right):
    return lax.dot_general(
        left, right, (((0,), (0,)), ((), ())), preferred_element_type=jnp.float32
    )


def inverse_norm(sumsq):
    return lax.rsqrt(jnp.where(sumsq > 0.0, sumsq, 1.0))


def as_columns(row, width):
    return jnp.broadcast_to(row, (width, row.shape[1])).T


def mirrored_lower(square):
    rows = lax.broadcasted_iota(jnp.int32, square.shape, 0)
    columns = lax.broadcasted_iota(jnp.int32, square.shape, 1)
    return jnp.where(rows >= columns, square, square.T)


def to_fixed(values):
    return jnp.round(values * UNIT).astype(jnp.int32).astype(jnp.int16)


def coded(norm):
    exponent = jnp.floor(jnp.log2(jnp.where(norm > 0.0, norm, 1.0)))
    mantissa = norm * jnp.exp2(-exponent) * 8192.0
    high = jnp.floor(mantissa)
    low = jnp.floor((mantissa - high) * 16384.0 + 0.5)
    rows = lax.broadcasted_iota(jnp.int32, (CODE_ROWS, norm.shape[1]), 0)
    values = jnp.where(rows == 0, high, jnp.where(rows == 1, low, exponent))
    return jnp.where(rows < 3, values, 0.0).astype(jnp.int32).astype(jnp.int16)


def decoded(rows):
    rows = rows.astype(jnp.int32).astype(jnp.float32)
    mantissa = (rows[0:1] + rows[1:2] * (1.0 / 16384.0)) * (1.0 / 8192.0)
    return mantissa * jnp.exp2(rows[2:3])


def adjusted(corr, count_all):
    squared = corr * corr
    return squared - (1.0 - squared) / (count_all - 2.0)


def kernel_call(kernel, out_shape, operands, in_specs=None, grid=None, scratch=()):
    in_specs = in_specs or [None] * len(operands)
    whole = pl.BlockSpec(memory_space=pltpu.VMEM)
    extra = {} if grid is None else {"grid": grid}
    return pl.pallas_call(
        kernel,
        out_shape=out_shape,
        in_specs=[spec or whole for spec in in_specs],
        scratch_shapes=list(scratch),
        compiler_params=pltpu.CompilerParams(vmem_limit_bytes=36 * 1024 * 1024),
        **extra,
    )(*operands)


def write_slabs(place, values, slabs):
    rows = values.shape[0] // len(slabs)
    for by, slab in enumerate(slabs):
        first = lax.rem(place + by, len(slabs)) * rows
        slab[:rows] = to_fixed(values[pl.ds(pl.multiple_of(first, 16), rows), :])


def own_kernel(groups, place, array, second, scale, *rest):
    slabs, values = rest[:groups], rest[groups]
    second[...] = array[:, second.shape[1] :]
    squares = column_squares(array[...])
    inverse = inverse_norm(squares)
    scale[...] = inverse
    product = transposed_product(array[...], array[...])
    columns = as_columns(inverse, LANES)
    columns = jnp.concatenate([columns] * (product.shape[1] // LANES), axis=1)
    values[...] = product * columns * inverse
    write_slabs(place[0], values, slabs)
    code = coded(squares * inverse)
    for slab in slabs:
        slab[-CODE_ROWS:] = code


def scaled_product(left, right, left_scale):
    right_scale = inverse_norm(column_squares(right))
    product = transposed_product(left, right)
    columns = as_columns(left_scale, LANES)
    columns = jnp.concatenate([columns] * (product.shape[1] // LANES), axis=1)
    return product * columns * right_scale


def first_kernel(groups, place, left, right, left_scale, corner, *rest):
    slabs, values = rest[:groups], rest[groups]
    half = right.shape[1]
    product = scaled_product(left[...], right[...], left_scale[...])
    values[:half] = mirrored_lower(product[:half])
    values[half:] = product[half:]
    corner[...] = product[half:]
    write_slabs(place[0], values, slabs)


def second_kernel(groups, place, left, right, left_scale, corner, *rest):
    slabs, values = rest[:groups], rest[groups]
    half = right.shape[1]
    values[:half] = corner[...].T
    values[half:] = mirrored_lower(scaled_product(left[...], right[...], left_scale[...]))
    write_slabs(place[0], values, slabs)


def shares_kernel(groups, starts, *rest):
    terms, (rows, columns) = rest[:groups], rest[groups:]
    norms = [decoded(term[...]) for term in terms]
    sumsq = functools.reduce(jnp.add, [norm * norm for norm in norms])
    inverse = inverse_norm(sumsq)
    rows[...] = jnp.zeros(rows.shape, jnp.float32)
    for by, norm in enumerate(norms):
        rows[by : by + 1, :] = norm * inverse
    rows[groups : groups + 1, : starts.shape[1]] = starts[...].astype(jnp.float32)
    rows[groups + 1 : groups + 2, :] = sumsq * lax.rsqrt(sumsq) * inverse
    fill = jnp.zeros((LANES - rows.shape[0], rows.shape[1]), jnp.float32)
    columns[...] = jnp.concatenate([rows[...], fill], axis=0).T


def per_device(genotypes, annotations, window_start, window_end):
    stripe = genotypes.shape[1]
    half = stripe // 2
    groups = lax.axis_size("ind")
    count_all = float(genotypes.shape[0] * groups)
    sub_rows = stripe // groups
    place = lax.axis_index("ind").astype(jnp.int32)
    place = jnp.stack([place, lax.axis_index("snp").astype(jnp.int32) * stripe])
    scalar = pl.BlockSpec(memory_space=pltpu.SMEM)

    def shape(*dims, dtype=jnp.float32):
        return jax.ShapeDtypeStruct(dims, dtype)

    def slab_shapes(rows, columns):
        return (shape(rows, columns, dtype=jnp.int16),) * groups

    above_first = shifted(genotypes[:, :half], "snp", -1)
    second, scale, *own_slabs = kernel_call(
        functools.partial(own_kernel, groups),
        (
            shape(genotypes.shape[0], half, dtype=genotypes.dtype),
            shape(1, stripe),
            *slab_shapes(sub_rows + CODE_ROWS, stripe),
        ),
        (place, genotypes),
        [scalar, None],
        scratch=[pltpu.VMEM((stripe, stripe), jnp.float32)],
    )
    own_terms = exchanged(own_slabs, "ind")
    above_second = shifted(after(second, scale), "snp", -1)

    corner, *first_slabs = kernel_call(
        functools.partial(first_kernel, groups),
        (shape(half, half), *slab_shapes(sub_rows, half)),
        (place, genotypes, above_first, scale),
        [scalar, None, None, None],
        scratch=[pltpu.VMEM((stripe, half), jnp.float32)],
    )
    first_terms = exchanged([after(slab, own_terms[2]) for slab in first_slabs], "ind")
    annot_above = shifted(after(annotations, scale), "snp", -1)

    code = pl.BlockSpec((CODE_ROWS, stripe), lambda i: (sub_rows // CODE_ROWS, 0))
    info_rows = -(-(groups + 2) // 8) * 8
    shares, share_columns = kernel_call(
        functools.partial(shares_kernel, groups),
        (shape(info_rows, stripe), shape(stripe, LANES)),
        (window_start[None], *(after(term, corner) for term in own_terms)),
        [None] + [code] * groups,
        grid=(1,),
    )
    above = shifted(shares, "snp", -1)

    above_second = after(above_second, shares, first_terms[1])
    second_slabs = kernel_call(
        functools.partial(second_kernel, groups),
        slab_shapes(sub_rows, half),
        (place, genotypes, above_second, scale, corner),
        [
            scalar,
            pl.BlockSpec((genotypes.shape[0], half), lambda i: (0, 1)),
            None,
            pl.BlockSpec((1, half), lambda i: (0, 1)),
            None,
        ],
        grid=(1,),
        scratch=[pltpu.VMEM((stripe, half), jnp.float32)],
    )
    second_terms = exchanged(second_slabs, "ind")

    def rows_of(array):
        return lax.dynamic_slice_in_dim(array, place[0] * sub_rows, sub_rows, 0)

    ids = jnp.arange(stripe, dtype=jnp.int32)[None, :]
    row_ids = place[0] * sub_rows + jnp.arange(sub_rows, dtype=jnp.int32)[:, None]
    lower = row_ids >= ids
    own_ids = place[1] + ids
    here = rows_of(share_columns)
    next_here = rows_of(above.T)

    def column(array, by):
        return array[:, by : by + 1]

    def row(array, by):
        return array[by : by + 1, :]

    own_corr = sum(
        term[:sub_rows].astype(jnp.float32) * column(here, by) * row(shares, by)
        for by, term in enumerate(own_terms)
    )
    own_corr = own_corr * (1.0 / UNIT) * column(here, groups + 1)
    inside = (own_ids >= window_start[:, None]) & (own_ids < window_end[:, None])
    own_weights = jnp.where(inside, adjusted(own_corr, count_all), 0.0).astype(jnp.bfloat16)
    score = jnp.dot(own_weights, annotations, preferred_element_type=jnp.float32)

    cross_corr = 0.0
    for by in range(groups):
        term = jnp.concatenate([first_terms[by], second_terms[by]], axis=1).astype(jnp.float32)
        below = column(here, by) * row(above, by)
        cross_corr += term * jnp.where(lower, below, column(next_here, by) * row(shares, by))
    cross_weights = adjusted(cross_corr * (1.0 / UNIT), count_all).astype(jnp.bfloat16)
    start_above = above[groups, :sub_rows].astype(jnp.int32)
    inside = (own_ids >= start_above[:, None]) & (ids >= row_ids)
    mirrored = jnp.where(inside, cross_weights, 0)
    mirrored = jnp.dot(mirrored, annotations, preferred_element_type=jnp.float32)
    mirrored = shifted(mirrored.astype(jnp.bfloat16), "snp", 1)

    inside = (own_ids + stripe < window_end[:, None]) & lower
    above_weights = jnp.where(inside, cross_weights, 0)
    score += jnp.dot(above_weights, annot_above, preferred_element_type=jnp.float32)
    return score + mirrored.astype(jnp.float32)


def solution(mesh):
    in_specs = (P("ind", "snp"), P("snp", None), P(("snp", "ind")), P(("snp", "ind")))
    out_specs = P(("snp", "ind"), None)
    return jax.shard_map(
        per_device, mesh=mesh, in_specs=in_specs, out_specs=out_specs, check_vma=False
    )
```

```python
import functools

import jax
import jax.numpy as jnp
from jax import lax
from jax.experimental import pallas as pl
from jax.experimental.pallas import tpu as pltpu
from jax.sharding import PartitionSpec as P

UNIT = 32000.0
LANES = 128
CODE_ROWS = 8


def shifted(array, axis, by):
    devices = lax.axis_size(axis)
    pairs = [(i, i + by) for i in range(devices) if 0 <= i + by < devices]
    return lax.ppermute(array, axis, pairs)


def after(value, *earlier):
    return lax.optimization_barrier((value, *earlier))[0]


def exchanged(slabs, axis):
    devices = lax.axis_size(axis)
    terms = [slabs[0]] * devices
    for by in reversed(range(1, devices)):
        pairs = [(i, (i + by) % devices) for i in range(devices)]
        terms[by] = lax.ppermute(slabs[by], axis, pairs)
    return terms


def column_squares(block):
    widened = block.astype(jnp.float32)
    return jnp.sum(widened * widened, axis=0, keepdims=True)


def transposed_product(left, right):
    return lax.dot_general(
        left, right, (((0,), (0,)), ((), ())), preferred_element_type=jnp.float32
    )


def inverse_norm(sumsq):
    return lax.rsqrt(jnp.where(sumsq > 0.0, sumsq, 1.0))


def as_columns(row, width):
    return jnp.broadcast_to(row, (width, row.shape[1])).T


def mirrored_lower(square):
    rows = lax.broadcasted_iota(jnp.int32, square.shape, 0)
    columns = lax.broadcasted_iota(jnp.int32, square.shape, 1)
    return jnp.where(rows >= columns, square, square.T)


def to_fixed(values):
    return jnp.round(values * UNIT).astype(jnp.int32).astype(jnp.int16)


def coded(norm):
    exponent = jnp.floor(jnp.log2(jnp.where(norm > 0.0, norm, 1.0)))
    mantissa = norm * jnp.exp2(-exponent) * 8192.0
    high = jnp.floor(mantissa)
    low = jnp.floor((mantissa - high) * 16384.0 + 0.5)
    rows = lax.broadcasted_iota(jnp.int32, (CODE_ROWS, norm.shape[1]), 0)
    values = jnp.where(rows == 0, high, jnp.where(rows == 1, low, exponent))
    return jnp.where(rows < 3, values, 0.0).astype(jnp.int32).astype(jnp.int16)


def decoded(rows):
    rows = rows.astype(jnp.int32).astype(jnp.float32)
    mantissa = (rows[0:1] + rows[1:2] * (1.0 / 16384.0)) * (1.0 / 8192.0)
    return mantissa * jnp.exp2(rows[2:3])


def adjusted(corr, count_all):
    squared = corr * corr
    return squared - (1.0 - squared) / (count_all - 2.0)


def kernel_call(kernel, out_shape, operands, in_specs=None, grid=None, scratch=()):
    in_specs = in_specs or [None] * len(operands)
    whole = pl.BlockSpec(memory_space=pltpu.VMEM)
    extra = {} if grid is None else {"grid": grid}
    return pl.pallas_call(
        kernel,
        out_shape=out_shape,
        in_specs=[spec or whole for spec in in_specs],
        scratch_shapes=list(scratch),
        compiler_params=pltpu.CompilerParams(vmem_limit_bytes=36 * 1024 * 1024),
        **extra,
    )(*operands)


def write_slabs(place, values, slabs):
    rows = values.shape[0] // len(slabs)
    for by, slab in enumerate(slabs):
        first = lax.rem(place + by, len(slabs)) * rows
        slab[:rows] = to_fixed(values[pl.ds(pl.multiple_of(first, 16), rows), :])


def own_kernel(groups, place, array, second, scale, *rest):
    slabs, values = rest[:groups], rest[groups]
    second[...] = array[:, second.shape[1] :]
    squares = column_squares(array[...])
    inverse = inverse_norm(squares)
    scale[...] = inverse
    product = transposed_product(array[...], array[...])
    columns = as_columns(inverse, LANES)
    columns = jnp.concatenate([columns] * (product.shape[1] // LANES), axis=1)
    values[...] = product * columns * inverse
    write_slabs(place[0], values, slabs)
    code = coded(squares * inverse)
    for slab in slabs:
        slab[-CODE_ROWS:] = code


def scaled_product(left, right, left_scale):
    right_scale = inverse_norm(column_squares(right))
    product = transposed_product(left, right)
    columns = as_columns(left_scale, LANES)
    columns = jnp.concatenate([columns] * (product.shape[1] // LANES), axis=1)
    return product * columns * right_scale


def first_kernel(groups, place, left, right, left_scale, corner, *rest):
    slabs, values = rest[:groups], rest[groups]
    half = right.shape[1]
    product = scaled_product(left[...], right[...], left_scale[...])
    values[:half] = mirrored_lower(product[:half])
    values[half:] = product[half:]
    corner[...] = product[half:]
    write_slabs(place[0], values, slabs)


def second_kernel(groups, place, left, right, left_scale, corner, *rest):
    slabs, values = rest[:groups], rest[groups]
    half = right.shape[1]
    values[:half] = corner[...].T
    product = scaled_product(left[:, half:], right[...], left_scale[:, half:])
    values[half:] = mirrored_lower(product)
    write_slabs(place[0], values, slabs)


def shares_kernel(groups, starts, *rest):
    terms, (rows, columns) = rest[:groups], rest[groups:]
    norms = [decoded(term[...]) for term in terms]
    sumsq = functools.reduce(jnp.add, [norm * norm for norm in norms])
    inverse = inverse_norm(sumsq)
    rows[...] = jnp.zeros(rows.shape, jnp.float32)
    for by, norm in enumerate(norms):
        rows[by : by + 1, :] = norm * inverse
    rows[groups : groups + 1, : starts.shape[1]] = starts[...].astype(jnp.float32)
    rows[groups + 1 : groups + 2, :] = sumsq * lax.rsqrt(sumsq) * inverse
    fill = jnp.zeros((LANES - rows.shape[0], rows.shape[1]), jnp.float32)
    columns[...] = jnp.concatenate([rows[...], fill], axis=0).T


def per_device(genotypes, annotations, window_start, window_end):
    stripe = genotypes.shape[1]
    half = stripe // 2
    groups = lax.axis_size("ind")
    count_all = float(genotypes.shape[0] * groups)
    sub_rows = stripe // groups
    place = lax.axis_index("ind").astype(jnp.int32)
    place = jnp.stack([place, lax.axis_index("snp").astype(jnp.int32) * stripe])
    scalar = pl.BlockSpec(memory_space=pltpu.SMEM)

    def shape(*dims, dtype=jnp.float32):
        return jax.ShapeDtypeStruct(dims, dtype)

    def slab_shapes(rows, columns):
        return (shape(rows, columns, dtype=jnp.int16),) * groups

    above_first = shifted(genotypes[:, :half], "snp", -1)
    second, scale, *own_slabs = kernel_call(
        functools.partial(own_kernel, groups),
        (
            shape(genotypes.shape[0], half, dtype=genotypes.dtype),
            shape(1, stripe),
            *slab_shapes(sub_rows + CODE_ROWS, stripe),
        ),
        (place, genotypes),
        [scalar, None],
        scratch=[pltpu.VMEM((stripe, stripe), jnp.float32)],
    )
    own_terms = exchanged(own_slabs, "ind")
    above_second = shifted(after(second, scale), "snp", -1)

    corner, *first_slabs = kernel_call(
        functools.partial(first_kernel, groups),
        (shape(half, half), *slab_shapes(sub_rows, half)),
        (place, genotypes, above_first, scale),
        [scalar, None, None, None],
        scratch=[pltpu.VMEM((stripe, half), jnp.float32)],
    )
    first_terms = exchanged([after(slab, own_terms[2]) for slab in first_slabs], "ind")
    annot_above = shifted(after(annotations, scale), "snp", -1)

    code = pl.BlockSpec((CODE_ROWS, stripe), lambda i: (sub_rows // CODE_ROWS, 0))
    info_rows = -(-(groups + 2) // 8) * 8
    shares, share_columns = kernel_call(
        functools.partial(shares_kernel, groups),
        (shape(info_rows, stripe), shape(stripe, LANES)),
        (window_start[None], *(after(term, corner) for term in own_terms)),
        [None] + [code] * groups,
        grid=(1,),
    )
    above = shifted(shares, "snp", -1)

    above_second = after(above_second, shares, first_terms[1])
    second_slabs = kernel_call(
        functools.partial(second_kernel, groups),
        slab_shapes(sub_rows, half),
        (place, genotypes, above_second, scale, corner),
        [scalar, None, None, None, None],
        scratch=[pltpu.VMEM((stripe, half), jnp.float32)],
    )
    second_terms = exchanged(second_slabs, "ind")

    def rows_of(array):
        return lax.dynamic_slice_in_dim(array, place[0] * sub_rows, sub_rows, 0)

    ids = jnp.arange(stripe, dtype=jnp.int32)[None, :]
    row_ids = place[0] * sub_rows + jnp.arange(sub_rows, dtype=jnp.int32)[:, None]
    lower = row_ids >= ids
    own_ids = place[1] + ids
    here = rows_of(share_columns)
    next_here = rows_of(above.T)

    def column(array, by):
        return array[:, by : by + 1]

    def row(array, by):
        return array[by : by + 1, :]

    own_corr = sum(
        term[:sub_rows].astype(jnp.float32) * column(here, by) * row(shares, by)
        for by, term in enumerate(own_terms)
    )
    own_corr = own_corr * (1.0 / UNIT) * column(here, groups + 1)
    inside = (own_ids >= window_start[:, None]) & (own_ids < window_end[:, None])
    own_weights = jnp.where(inside, adjusted(own_corr, count_all), 0.0).astype(jnp.bfloat16)
    score = jnp.dot(own_weights, annotations, preferred_element_type=jnp.float32)

    cross_corr = 0.0
    for by in range(groups):
        term = jnp.concatenate([first_terms[by], second_terms[by]], axis=1).astype(jnp.float32)
        below = column(here, by) * row(above, by)
        cross_corr += term * jnp.where(lower, below, column(next_here, by) * row(shares, by))
    cross_weights = adjusted(cross_corr * (1.0 / UNIT), count_all).astype(jnp.bfloat16)
    start_above = above[groups, :sub_rows].astype(jnp.int32)
    inside = (own_ids >= start_above[:, None]) & (ids >= row_ids)
    mirrored = jnp.where(inside, cross_weights, 0)
    mirrored = jnp.dot(mirrored, annotations, preferred_element_type=jnp.float32)
    mirrored = shifted(mirrored.astype(jnp.bfloat16), "snp", 1)

    inside = (own_ids + stripe < window_end[:, None]) & lower
    above_weights = jnp.where(inside, cross_weights, 0)
    score += jnp.dot(above_weights, annot_above, preferred_element_type=jnp.float32)
    return score + mirrored.astype(jnp.float32)


def solution(mesh):
    in_specs = (P("ind", "snp"), P("snp", None), P(("snp", "ind")), P(("snp", "ind")))
    out_specs = P(("snp", "ind"), None)
    return jax.shard_map(
        per_device, mesh=mesh, in_specs=in_specs, out_specs=out_specs, check_vma=False
    )
```

```python
import functools

import jax
import jax.numpy as jnp
from jax import lax
from jax.experimental import pallas as pl
from jax.experimental.pallas import tpu as pltpu
from jax.sharding import PartitionSpec as P

UNIT = 32000.0
LANES = 128
CODE_ROWS = 8


def shifted(array, axis, by):
    devices = lax.axis_size(axis)
    pairs = [(i, i + by) for i in range(devices) if 0 <= i + by < devices]
    return lax.ppermute(array, axis, pairs)


def after(value, *earlier):
    return lax.optimization_barrier((value, *earlier))[0]


def exchanged(slabs, axis):
    devices = lax.axis_size(axis)
    terms = [slabs[0]] * devices
    for by in reversed(range(1, devices)):
        pairs = [(i, (i + by) % devices) for i in range(devices)]
        terms[by] = lax.ppermute(slabs[by], axis, pairs)
    return terms


def column_squares(block):
    widened = block.astype(jnp.float32)
    return jnp.sum(widened * widened, axis=0, keepdims=True)


def transposed_product(left, right):
    return lax.dot_general(
        left, right, (((0,), (0,)), ((), ())), preferred_element_type=jnp.float32
    )


def inverse_norm(sumsq):
    return lax.rsqrt(jnp.where(sumsq > 0.0, sumsq, 1.0))


def as_columns(row, width):
    return jnp.broadcast_to(row, (width, row.shape[1])).T


def mirrored_lower(square):
    rows = lax.broadcasted_iota(jnp.int32, square.shape, 0)
    columns = lax.broadcasted_iota(jnp.int32, square.shape, 1)
    return jnp.where(rows >= columns, square, square.T)


def to_fixed(values):
    return jnp.round(values * UNIT).astype(jnp.int32).astype(jnp.int16)


def coded(norm):
    exponent = jnp.floor(jnp.log2(jnp.where(norm > 0.0, norm, 1.0)))
    mantissa = norm * jnp.exp2(-exponent) * 8192.0
    high = jnp.floor(mantissa)
    low = jnp.floor((mantissa - high) * 16384.0 + 0.5)
    rows = lax.broadcasted_iota(jnp.int32, (CODE_ROWS, norm.shape[1]), 0)
    values = jnp.where(rows == 0, high, jnp.where(rows == 1, low, exponent))
    return jnp.where(rows < 3, values, 0.0).astype(jnp.int32).astype(jnp.int16)


def decoded(rows):
    rows = rows.astype(jnp.int32).astype(jnp.float32)
    mantissa = (rows[0:1] + rows[1:2] * (1.0 / 16384.0)) * (1.0 / 8192.0)
    return mantissa * jnp.exp2(rows[2:3])


def adjusted(corr, count_all):
    squared = corr * corr
    return squared - (1.0 - squared) / (count_all - 2.0)


def kernel_call(kernel, out_shape, operands, in_specs=None, grid=None, scratch=()):
    in_specs = in_specs or [None] * len(operands)
    whole = pl.BlockSpec(memory_space=pltpu.VMEM)
    extra = {} if grid is None else {"grid": grid}
    return pl.pallas_call(
        kernel,
        out_shape=out_shape,
        in_specs=[spec or whole for spec in in_specs],
        scratch_shapes=list(scratch),
        compiler_params=pltpu.CompilerParams(vmem_limit_bytes=36 * 1024 * 1024),
        **extra,
    )(*operands)


def write_slabs(place, values, slabs):
    rows = values.shape[0] // len(slabs)
    for by, slab in enumerate(slabs):
        first = lax.rem(place + by, len(slabs)) * rows
        slab[:rows] = to_fixed(values[pl.ds(pl.multiple_of(first, 16), rows), :])


def own_kernel(groups, place, array, second, scale, *rest):
    slabs, values = rest[:groups], rest[groups]
    second[...] = array[:, second.shape[1] :]
    squares = column_squares(array[...])
    inverse = inverse_norm(squares)
    scale[...] = inverse
    product = transposed_product(array[...], array[...])
    columns = as_columns(inverse, LANES)
    columns = jnp.concatenate([columns] * (product.shape[1] // LANES), axis=1)
    values[...] = product * columns * inverse
    write_slabs(place[0], values, slabs)
    code = coded(squares * inverse)
    for slab in slabs:
        slab[-CODE_ROWS:] = code


def scaled_product(left, right, left_scale):
    right_scale = inverse_norm(column_squares(right))
    product = transposed_product(left, right)
    columns = as_columns(left_scale, LANES)
    columns = jnp.concatenate([columns] * (product.shape[1] // LANES), axis=1)
    return product * columns * right_scale


def first_kernel(groups, place, left, right, left_scale, corner, *rest):
    slabs, values = rest[:groups], rest[groups]
    half = right.shape[1]
    product = scaled_product(left[...], right[...], left_scale[...])
    values[:half] = mirrored_lower(product[:half])
    values[half:] = product[half:]
    corner[...] = product[half:]
    write_slabs(place[0], values, slabs)


def second_kernel(groups, place, left, right, left_scale, corner, *rest):
    slabs, values = rest[:groups], rest[groups]
    half = right.shape[1]
    values[:half] = corner[...].T
    values[half:] = mirrored_lower(scaled_product(left[...], right[...], left_scale[...]))
    write_slabs(place[0], values, slabs)


def shares_kernel(groups, starts, *rest):
    terms, (rows, columns) = rest[:groups], rest[groups:]
    norms = [decoded(term[...]) for term in terms]
    sumsq = functools.reduce(jnp.add, [norm * norm for norm in norms])
    inverse = inverse_norm(sumsq)
    rows[...] = jnp.zeros(rows.shape, jnp.float32)
    for by, norm in enumerate(norms):
        rows[by : by + 1, :] = norm * inverse
    rows[groups : groups + 1, : starts.shape[1]] = starts[...].astype(jnp.float32)
    rows[groups + 1 : groups + 2, :] = sumsq * lax.rsqrt(sumsq) * inverse
    fill = jnp.zeros((LANES - rows.shape[0], rows.shape[1]), jnp.float32)
    columns[...] = jnp.concatenate([rows[...], fill], axis=0).T


def per_device(genotypes, annotations, window_start, window_end):
    stripe = genotypes.shape[1]
    half = stripe // 2
    groups = lax.axis_size("ind")
    count_all = float(genotypes.shape[0] * groups)
    sub_rows = stripe // groups
    place = lax.axis_index("ind").astype(jnp.int32)
    place = jnp.stack([place, lax.axis_index("snp").astype(jnp.int32) * stripe])
    scalar = pl.BlockSpec(memory_space=pltpu.SMEM)

    def shape(*dims, dtype=jnp.float32):
        return jax.ShapeDtypeStruct(dims, dtype)

    def slab_shapes(rows, columns):
        return (shape(rows, columns, dtype=jnp.int16),) * groups

    above_first = shifted(genotypes[:, :half], "snp", -1)
    second, scale, *own_slabs = kernel_call(
        functools.partial(own_kernel, groups),
        (
            shape(genotypes.shape[0], half, dtype=genotypes.dtype),
            shape(1, stripe),
            *slab_shapes(sub_rows + CODE_ROWS, stripe),
        ),
        (place, genotypes),
        [scalar, None],
        scratch=[pltpu.VMEM((stripe, stripe), jnp.float32)],
    )
    own_terms = exchanged(own_slabs, "ind")
    above_second = shifted(after(second, scale), "snp", -1)

    corner, *first_slabs = kernel_call(
        functools.partial(first_kernel, groups),
        (shape(half, half), *slab_shapes(sub_rows, half)),
        (place, genotypes, above_first, scale),
        [scalar, None, None, None],
        scratch=[pltpu.VMEM((stripe, half), jnp.float32)],
    )
    first_terms = exchanged([after(slab, own_terms[2]) for slab in first_slabs], "ind")
    annot_above = shifted(after(annotations, scale), "snp", -1)

    code = pl.BlockSpec((CODE_ROWS, stripe), lambda i: (sub_rows // CODE_ROWS, 0))
    info_rows = -(-(groups + 2) // 8) * 8
    shares, share_columns = kernel_call(
        functools.partial(shares_kernel, groups),
        (shape(info_rows, stripe), shape(stripe, LANES)),
        (window_start[None], *(after(term, corner) for term in own_terms)),
        [None] + [code] * groups,
        grid=(1,),
    )
    above = shifted(shares, "snp", -1)

    above_second = after(above_second, shares, first_terms[1])
    second_slabs = kernel_call(
        functools.partial(second_kernel, groups),
        slab_shapes(sub_rows, half),
        (place, genotypes, above_second, scale, corner),
        [
            scalar,
            pl.BlockSpec((genotypes.shape[0], half), lambda i: (0, 1)),
            None,
            pl.BlockSpec((1, half), lambda i: (0, 1)),
            None,
        ],
        grid=(1,),
        scratch=[pltpu.VMEM((stripe, half), jnp.float32)],
    )
    second_terms = exchanged(second_slabs, "ind")

    def rows_of(array):
        return lax.dynamic_slice_in_dim(array, place[0] * sub_rows, sub_rows, 0)

    ids = jnp.arange(stripe, dtype=jnp.int32)[None, :]
    row_ids = place[0] * sub_rows + jnp.arange(sub_rows, dtype=jnp.int32)[:, None]
    lower = row_ids >= ids
    own_ids = place[1] + ids
    here = rows_of(share_columns)
    next_here = rows_of(above.T)

    def column(array, by):
        return array[:, by : by + 1]

    def row(array, by):
        return array[by : by + 1, :]

    own_corr = sum(
        term[:sub_rows].astype(jnp.float32) * column(here, by) * row(shares, by)
        for by, term in enumerate(own_terms)
    )
    own_corr = own_corr * (1.0 / UNIT) * column(here, groups + 1)
    inside = (own_ids >= window_start[:, None]) & (own_ids < window_end[:, None])
    own_weights = jnp.where(inside, adjusted(own_corr, count_all), 0.0).astype(jnp.bfloat16)
    score = jnp.dot(own_weights, annotations, preferred_element_type=jnp.float32)

    cross_corr = 0.0
    for by in range(groups):
        term = jnp.concatenate([first_terms[by], second_terms[by]], axis=1).astype(jnp.float32)
        below = column(here, by) * row(above, by)
        cross_corr += term * jnp.where(lower, below, column(next_here, by) * row(shares, by))
    cross_weights = adjusted(cross_corr * (1.0 / UNIT), count_all).astype(jnp.bfloat16)
    start_above = above[groups, :sub_rows].astype(jnp.int32)
    inside = (own_ids >= start_above[:, None]) & (ids >= row_ids)
    mirrored = jnp.where(inside, cross_weights, 0)
    mirrored = jnp.dot(mirrored, annotations, preferred_element_type=jnp.float32)
    mirrored = shifted(mirrored.astype(jnp.bfloat16), "snp", 1)

    inside = (own_ids + stripe < window_end[:, None]) & lower
    above_weights = jnp.where(inside, cross_weights, 0)
    score += jnp.dot(above_weights, annot_above, preferred_element_type=jnp.float32)
    return score + mirrored.astype(jnp.float32)


def solution(mesh):
    in_specs = (P("ind", "snp"), P("snp", None), P(("snp", "ind")), P(("snp", "ind")))
    out_specs = P(("snp", "ind"), None)
    return jax.shard_map(
        per_device, mesh=mesh, in_specs=in_specs, out_specs=out_specs, check_vma=False
    )
```
